512 devices in a mesh: lag: 16 (over y, x_hi), row: 32 (over z, x_lo, core).
Axes of the slice: x: 4 (x_hi: 2, x_lo: 2; x = x_hi * 2 + x_lo), y: 8, z: 8, core: 2. Of those that a mesh axis runs over, the one named last changes fastest.
Arguments:
- newest: bfloat16 [512, 8192], P('lag', 'row'), may hold values from -6 to 6
- earlier: bfloat16 [15, 8192], P(None, 'row'), may hold values from -6 to 6
- lag_matrices: bfloat16 [16, 8192, 8192], P('lag', 'row'), may hold values from -0.015625 to 0.015625
Outputs:
- forces: float32 [512, 8192], P('lag', 'row')
The draws below stay inside these ranges and needn't reach their ends.
All inputs are finite; a program needn't handle non-finite values.
Results may differ from the reference program's by a relative error of at most 0.0003.
Values may be sent and summed in bfloat16 or wider, within the bound.
No kernel may reach another device: no remote copies, remote signals or barrier semaphores. Data moves between devices by JAX's collectives and lax.ppermute only.
A program may use at most 64 MiB of HBM per device.

```python
import jax
import jax.numpy as jnp
from jax import lax

DOF = 8192
STEPS = 512
LAGS = 16


def level_of(key, extent, shards, least, high):
    def one(position, shards_of):
        heights = jax.random.uniform(jax.random.fold_in(jax.random.fold_in(key, 6), position), (shards_of,), jnp.float32, least / len(shards), high / len(shards))
        return jnp.repeat(jnp.exp(heights), extent[position] // shards_of).reshape((-1,) + (1,) * (len(extent) - position - 1))

    level = one(*shards[0])
    for cut in shards[1:]:
        level = level * one(*cut)
    return level


def bell_draw(stream_key, extent, scale, bound, shards=(), held_as=jnp.bfloat16):
    drawn = jax.random.normal(stream_key, extent, jnp.float32) * scale
    if len(shards) > 0:
        drawn = level_of(stream_key, extent, shards, -0.22, 0.18) * drawn
    return jnp.clip(drawn, min=-bound, max=bound).astype(held_as)


def setup_inputs(seed: int = 0) -> dict:
    arg_keys = jax.random.split(jax.random.key(seed), 4)
    newest = bell_draw(arg_keys[0], (STEPS, DOF), 1.0, 6.0, ((0, 16), (1, 32)))
    earlier = bell_draw(arg_keys[1], (LAGS - 1, DOF), 1.0, 6.0, ((1, 32),))
    lag_matrices = bell_draw(arg_keys[2], (LAGS, DOF, DOF), (DOF * LAGS) ** -0.5, 0.015625, ((0, 16), (1, 32)))
    return dict(newest=newest, earlier=earlier, lag_matrices=lag_matrices)


def reference(newest, earlier, lag_matrices):
    record = jnp.concatenate([earlier, newest], axis=0)

    def add_lag(total, inputs):
        lag_number, matrix = inputs
        offset = (LAGS - 1 - lag_number).astype(jnp.int32)
        window = lax.dynamic_slice_in_dim(record, offset, STEPS, 0)
        return total + jnp.dot(window, matrix.T, preferred_element_type=jnp.float32), None

    zeros = jnp.zeros((STEPS, DOF), jnp.float32)
    lag_numbers = jnp.arange(LAGS).astype(jnp.int32)
    forces, unused = lax.scan(add_lag, zeros, (lag_numbers, lag_matrices))
    return forces
```

```python
import jax
import jax.numpy as jnp
from jax import lax
from jax.experimental import pallas as pl
from jax.experimental.pallas import tpu as pltpu
from jax.sharding import Mesh, PartitionSpec as P

AXES = ("yh", "yl", "h", "zh", "zl", "l", "c")
SIZES = (4, 2, 2, 4, 2, 2, 2)
LAG = ("yh", "yl", "h")
ROW = ("zh", "zl", "l", "c")
LIKE = ("yh", "h", "zh")

STEPS = 512
PAD = 16
WIDE = 256
BLOCK = 64
MESSAGE = 72
CHUNKS = 16
LIKES = 32
PACKED = LIKES * BLOCK + 4 * PAD


def device_index(x, y, z, c):
    x, y, z = x % 4, y % 8, z % 8
    return (((y * 2 + x // 2) * 8 + z) * 2 + x % 2) * 2 + c


def cubes():
    groups = []
    for c in range(2):
        for x in range(0, 4, 2):
            for y in range(0, 8, 2):
                for z in range(0, 8, 2):
                    pairs = [sorted((v - c, v - c + 1), key=lambda w: w % 2) for v in (x, y, z)]
                    groups.append(
                        [device_index(i, j, k, c) for i in pairs[0] for j in pairs[1] for k in pairs[2]]
                    )
    return groups


def product_kernel(first_row, history, matrix, out, total):
    for chunk in range(CHUNKS):
        zh, zl, l = chunk // 4, chunk // 2 % 2, chunk % 2

        def part(yl, start, rows):
            return history[l * 4 + yl * 2 + zl, start : start + rows, :]

        halves = []
        for half in range(2):
            rows = [part(half, LIKES * BLOCK + zh * PAD, PAD)]
            for yh in range(4):
                for yl in range(2):
                    for h in range(2):
                        like = (yh * 2 + h) * 4 + zh
                        rows.append(part(yl, like * BLOCK + half * 32, 32))
            halves.append(jnp.concatenate(rows, axis=0))
        term = lax.dot_general(
            jnp.concatenate(halves, axis=1),
            matrix[:, chunk * WIDE : (chunk + 1) * WIDE],
            (((1,), (1,)), ((), ())),
            preferred_element_type=jnp.float32,
        )
        total[...] = term if chunk == 0 else total[...] + term
    rows = STEPS + PAD
    out[...] = pltpu.roll(total[...], rows - first_row[0], 0)[:STEPS]


def product(first_row, history, matrix):
    return pl.pallas_call(
        product_kernel,
        out_shape=jax.ShapeDtypeStruct((STEPS, WIDE), jnp.float32),
        in_specs=[
            pl.BlockSpec(memory_space=pltpu.SMEM),
            pl.BlockSpec(memory_space=pltpu.VMEM),
            pl.BlockSpec(memory_space=pltpu.VMEM),
        ],
        out_specs=pl.BlockSpec(memory_space=pltpu.VMEM),
        scratch_shapes=[pltpu.VMEM((STEPS + PAD, WIDE), jnp.float32)],
        compiler_params=pltpu.CompilerParams(vmem_limit_bytes=40 * 1024 * 1024),
        cost_estimate=pl.CostEstimate(
            flops=2 * (STEPS + PAD) * WIDE * WIDE * CHUNKS, bytes_accessed=7 << 20, transcendentals=0
        ),
    )(first_row, history, matrix)


def on_device(newest, earlier, lag_matrices):
    index = {axis: lax.axis_index(axis) for axis in AXES}
    lag = (index["yh"] * 2 + index["yl"]) * 2 + index["h"]
    core = index["c"]
    swap = [(0, 1), (1, 0)]

    matrix = lag_matrices[0].reshape(WIDE, CHUNKS, 2, WIDE)
    given = lax.dynamic_index_in_dim(matrix, 1 - core, 2, keepdims=False).reshape(WIDE, CHUNKS * WIDE)
    kept = lax.dynamic_index_in_dim(matrix, core, 2, keepdims=False).reshape(WIDE, CHUNKS * WIDE)
    taken = lax.ppermute(given, "c", swap)

    padded = jnp.pad(earlier, ((1, 0), (0, 0)))
    rows = lax.dynamic_slice(padded, ((index["yh"] * 2 + index["h"]) * 2, index["yl"] * 128), (2, 128))
    block = newest.reshape(32, 2, 128).transpose(1, 0, 2).reshape(BLOCK, 128)
    message = jnp.concatenate([block, rows, jnp.zeros((MESSAGE - BLOCK - 2, 128), block.dtype)], axis=0)

    like = lax.all_to_all(jnp.broadcast_to(message[None], (LIKES, MESSAGE, 128)), LIKE, 0, 0, tiled=True)
    before = like[:, BLOCK : BLOCK + 2].reshape(8, 4, 2, 128).transpose(1, 0, 2, 3).reshape(4 * PAD, 128)
    packed = jnp.concatenate([like[:, :BLOCK].reshape(LIKES * BLOCK, 128), before], axis=0)
    history = lax.all_to_all(
        jnp.broadcast_to(packed[None], (8, PACKED, 128)), AXES, 0, 0, tiled=True, axis_index_groups=cubes()
    )

    first_row = (PAD - lag).astype(jnp.int32)[None]
    for_sibling = product(first_row, history, taken)
    from_sibling = lax.ppermute(for_sibling, "c", swap)
    terms = product(first_row, history, kept) + from_sibling
    terms = lax.all_to_all(terms.reshape(16, 32, WIDE), LAG, 0, 0, tiled=True)
    return jnp.sum(terms, axis=0)


def solution(mesh):
    fine = Mesh(mesh.devices.reshape(SIZES), AXES)
    in_specs = (P(LAG, ROW), P(None, ROW), P(LAG, ROW, None))
    return jax.shard_map(on_device, mesh=fine, in_specs=in_specs, out_specs=P(LAG, ROW), check_vma=False)
```

```python
import jax
import jax.numpy as jnp
from jax import lax
from jax.experimental import pallas as pl
from jax.experimental.pallas import tpu as pltpu
from jax.sharding import Mesh, PartitionSpec as P

AXES = ("yh", "yl", "h", "zh", "zl", "l", "c")
SIZES = (4, 2, 2, 4, 2, 2, 2)
LAG = ("yh", "yl", "h")
ROW = ("zh", "zl", "l", "c")
LIKE = ("yh", "h", "zh")

STEPS = 512
PAD = 16
WIDE = 256
BLOCK = 64
MESSAGE = 72
CHUNKS = 16
LIKES = 32
PACKED = LIKES * BLOCK + 4 * PAD


def device_index(x, y, z, c):
    x, y, z = x % 4, y % 8, z % 8
    return (((y * 2 + x // 2) * 8 + z) * 2 + x % 2) * 2 + c


def cubes():
    groups = []
    for c in range(2):
        for x in range(0, 4, 2):
            for y in range(0, 8, 2):
                for z in range(0, 8, 2):
                    pairs = [sorted((v - c, v - c + 1), key=lambda w: w % 2) for v in (x, y, z)]
                    groups.append(
                        [device_index(i, j, k, c) for i in pairs[0] for j in pairs[1] for k in pairs[2]]
                    )
    return groups


def lag_index():
    return (lax.axis_index("yh") * 2 + lax.axis_index("yl")) * 2 + lax.axis_index("h")


def product_kernel(history, matrix, out, total):
    first_row, core = PAD - lag_index(), lax.axis_index("c")
    for chunk in range(CHUNKS):
        zh, zl, l = chunk // 4, chunk // 2 % 2, chunk % 2

        def part(yl, start, rows):
            return history[l * 4 + yl * 2 + zl, start : start + rows, :]

        halves = []
        for half in range(2):
            rows = [part(half, LIKES * BLOCK + zh * PAD, PAD)]
            for yh in range(4):
                for yl in range(2):
                    for h in range(2):
                        like = (yh * 2 + h) * 4 + zh
                        rows.append(part(yl, like * BLOCK + half * 32, 32))
            halves.append(jnp.concatenate(rows, axis=0))
        term = lax.dot_general(
            jnp.concatenate(halves, axis=1),
            matrix[:, pl.ds(pl.multiple_of((2 * chunk + core) * WIDE, WIDE), WIDE)],
            (((1,), (1,)), ((), ())),
            preferred_element_type=jnp.float32,
        )
        total[...] = term if chunk == 0 else total[...] + term
    rows = STEPS + PAD
    out[...] = pltpu.roll(total[...], rows - first_row, 0)[:STEPS]


def product(history, matrix):
    return pl.pallas_call(
        product_kernel,
        out_shape=jax.ShapeDtypeStruct((STEPS, WIDE), jnp.float32),
        in_specs=[
            pl.BlockSpec(memory_space=pltpu.VMEM),
            pl.BlockSpec(memory_space=pltpu.VMEM),
        ],
        out_specs=pl.BlockSpec(memory_space=pltpu.VMEM),
        scratch_shapes=[pltpu.VMEM((STEPS + PAD, WIDE), jnp.float32)],
        compiler_params=pltpu.CompilerParams(vmem_limit_bytes=16 * 1024 * 1024),
        cost_estimate=pl.CostEstimate(
            flops=2 * (STEPS + PAD) * WIDE * WIDE * CHUNKS, bytes_accessed=7 << 20, transcendentals=0
        ),
    )(history, matrix)


def on_device(newest, earlier, lag_matrices):
    index = {axis: lax.axis_index(axis) for axis in AXES}
    swap = [(0, 1), (1, 0)]

    matrix = lag_matrices[0]
    sibling_matrix = lax.ppermute(matrix, "c", swap)

    padded = jnp.pad(earlier, ((1, 0), (0, 0)))
    rows = lax.dynamic_slice(padded, ((index["yh"] * 2 + index["h"]) * 2, index["yl"] * 128), (2, 128))
    block = newest.reshape(32, 2, 128).transpose(1, 0, 2).reshape(BLOCK, 128)
    message = jnp.concatenate([block, rows, jnp.zeros((MESSAGE - BLOCK - 2, 128), block.dtype)], axis=0)

    like = lax.all_to_all(jnp.broadcast_to(message[None], (LIKES, MESSAGE, 128)), LIKE, 0, 0, tiled=True)
    before = like[:, BLOCK : BLOCK + 2].reshape(8, 4, 2, 128).transpose(1, 0, 2, 3).reshape(4 * PAD, 128)
    packed = jnp.concatenate([like[:, :BLOCK].reshape(LIKES * BLOCK, 128), before], axis=0)
    packed = packed + 0 * sibling_matrix[0, 0]
    history = lax.all_to_all(
        jnp.broadcast_to(packed[None], (8, PACKED, 128)), AXES, 0, 0, tiled=True, axis_index_groups=cubes()
    )

    for_sibling = product(history, sibling_matrix)
    from_sibling = lax.ppermute(for_sibling, "c", swap)
    terms = product(history, matrix) + from_sibling
    terms = lax.all_to_all(terms.reshape(16, 32, WIDE), LAG, 0, 0, tiled=True)
    return jnp.sum(terms, axis=0)


def solution(mesh):
    fine = Mesh(mesh.devices.reshape(SIZES), AXES)
    in_specs = (P(LAG, ROW), P(None, ROW), P(LAG, ROW, None))
    return jax.shard_map(on_device, mesh=fine, in_specs=in_specs, out_specs=P(LAG, ROW), check_vma=False)
```

```python
import jax
import jax.numpy as jnp
from jax import lax
from jax.experimental import pallas as pl
from jax.experimental.pallas import tpu as pltpu
from jax.sharding import Mesh, PartitionSpec as P

AXES = ("yh", "yl", "h", "zh", "zl", "l", "c")
SIZES = (4, 2, 2, 4, 2, 2, 2)
LAG = ("yh", "yl", "h")
ROW = ("zh", "zl", "l", "c")

RINGS = (4, 8, 8)
STEPS = 512
OWN = 32
PAD = 16
WIDE = 256
HALF = 128
BLOCK = 64
MESSAGE = 72
CHUNKS = 16
LIKES = 32
PACKED = LIKES * BLOCK + 8 * PAD
VMEM = pl.BlockSpec(memory_space=pltpu.VMEM)


def split_ring(u, size):
    return u // 2, (u % 2 + u // (size // 2)) % 2


def join_ring(pair, side, size):
    return 2 * pair + (side + 2 * pair // (size // 2)) % 2


def device_index(pairs, sides, c):
    x, y, z = ((join_ring(p, s, n) - c) % n for p, s, n in zip(pairs, sides, RINGS))
    return (((y * 2 + x // 2) * 8 + z) * 2 + x % 2) * 2 + c


def groups_of(same_side):
    all_pairs = [(px, py, pz) for py in range(4) for px in range(2) for pz in range(4)]
    all_sides = [(ax, ay, az) for ax in range(2) for ay in range(2) for az in range(2)]
    if same_side:
        return [[device_index(p, s, c) for p in all_pairs] for c in range(2) for s in all_sides]
    return [[device_index(p, s, c) for s in all_sides] for c in range(2) for p in all_pairs]


def lag_index():
    return (lax.axis_index("yh") * 2 + lax.axis_index("yl")) * 2 + lax.axis_index("h")


def columns_of(chunk, core):
    start = (2 * chunk + core) * WIDE
    return pl.ds(start if isinstance(core, int) else pl.multiple_of(start, WIDE), WIDE)


def position():
    c = lax.axis_index("c")
    x = lax.axis_index("h") * 2 + lax.axis_index("l")
    y = lax.axis_index("yh") * 2 + lax.axis_index("yl")
    z = lax.axis_index("zh") * 2 + lax.axis_index("zl")
    return [split_ring((v + c) % n, n) for v, n in zip((x, y, z), RINGS)]


def message_kernel(newest, earlier, out):
    (_, ax), (py, ay), _ = position()
    before = earlier[...].astype(jnp.float32)
    row = lax.broadcasted_iota(jnp.int32, before.shape, 0) + 1
    mine = jnp.sum(jnp.where(row == ax * 8 + ay * 4 + py, before, 0.0), axis=0, keepdims=True)
    place = lax.broadcasted_iota(jnp.int32, (MESSAGE - BLOCK, HALF), 0)
    extra = jnp.where(place == 0, mine[:, :HALF], jnp.where(place == 1, mine[:, HALF:], 0.0))
    block = newest[...]
    out[...] = jnp.concatenate([block[:, :HALF], block[:, HALF:], extra.astype(block.dtype)], axis=0)


def message(newest, earlier):
    return pl.pallas_call(
        message_kernel,
        out_shape=jax.ShapeDtypeStruct((MESSAGE, HALF), newest.dtype),
        in_specs=[VMEM, VMEM],
        out_specs=VMEM,
    )(newest, earlier)


def pack_kernel(like, sibling_matrix, out, sibling_columns, arrived):
    copies = [
        pltpu.make_async_copy(
            sibling_matrix.at[:, columns_of(chunk, lax.axis_index("c"))],
            sibling_columns.at[:, chunk * WIDE : (chunk + 1) * WIDE],
            arrived.at[chunk],
        )
        for chunk in range(CHUNKS)
    ]
    for copy in copies:
        copy.start()
    _, (_, ay), _ = position()
    place = lax.broadcasted_iota(jnp.int32, (PAD, HALF), 0) - ay * 4
    for pz in range(4):
        for px in range(2):
            before = jnp.zeros((PAD, HALF), jnp.float32)
            for py in range(4):
                index = (py * 2 + px) * 4 + pz
                whole = like[index]
                for copy in range(8):
                    out[copy, index * BLOCK : (index + 1) * BLOCK, :] = whole[:BLOCK]
                extra = whole[BLOCK:].astype(jnp.float32)
                before = jnp.where(place == py, extra[0:1], jnp.where(place == 8 + py, extra[1:2], before))
            start = LIKES * BLOCK + (pz * 2 + px) * PAD
            for copy in range(8):
                out[copy, start : start + PAD, :] = before.astype(like.dtype)
    for copy in copies:
        copy.wait()


def pack(like, sibling_matrix):
    return pl.pallas_call(
        pack_kernel,
        out_shape=[
            jax.ShapeDtypeStruct((8, PACKED, HALF), like.dtype),
            jax.ShapeDtypeStruct((WIDE, CHUNKS * WIDE), like.dtype),
        ],
        in_specs=[VMEM, pl.BlockSpec(memory_space=pl.ANY)],
        out_specs=[VMEM, VMEM],
        scratch_shapes=[pltpu.SemaphoreType.DMA((CHUNKS,))],
        compiler_params=pltpu.CompilerParams(vmem_limit_bytes=16 * 1024 * 1024),
    )(like, sibling_matrix)


def add_products(core, whole, history, matrix, total):
    for chunk in range(CHUNKS):
        z, l = chunk // 2, chunk % 2
        pz, az = split_ring((z + core) % 8, 8)
        halves = [[], []]
        before = []
        for h in range(2):
            px, ax = split_ring((2 * h + l + core) % 4, 4)
            start = LIKES * BLOCK + (pz * 2 + px) * PAD
            both = [history[ax * 4 + ay * 2 + az, start : start + PAD, :].astype(jnp.float32) for ay in range(2)]
            before.append((ax, both[0] + both[1]))
        before = [rows for _, rows in sorted(before, key=lambda entry: entry[0])]
        for half in range(2):
            rows = slice(half * 8, half * 8 + 8)
            halves[half].append(jnp.concatenate([before[0][rows], before[1][rows]], axis=0).astype(history.dtype))
        for y in range(8):
            py, ay = split_ring((y + core) % 8, 8)
            for h in range(2):
                px, ax = split_ring((2 * h + l + core) % 4, 4)
                start = ((py * 2 + px) * 4 + pz) * BLOCK
                for half in range(2):
                    first = start + half * OWN
                    halves[half].append(history[ax * 4 + ay * 2 + az, first : first + OWN, :])
        columns = columns_of(chunk, core) if whole else slice(chunk * WIDE, (chunk + 1) * WIDE)
        term = lax.dot_general(
            jnp.concatenate([jnp.concatenate(rows, axis=0) for rows in halves], axis=1),
            matrix[:, columns],
            (((1,), (1,)), ((), ())),
            preferred_element_type=jnp.float32,
        )
        total[...] = term if chunk == 0 else total[...] + term


def product_kernel(whole, history, matrix, out, total):
    for core in range(2):

        @pl.when(lax.axis_index("c") == core)
        def _():
            add_products(core, whole, history, matrix, total)

    rows = STEPS + PAD
    out[...] = pltpu.roll(total[...], rows - PAD + lag_index(), 0)[:STEPS]


def product(history, matrix):
    def kernel(*refs):
        product_kernel(matrix.shape[1] > CHUNKS * WIDE, *refs)

    return pl.pallas_call(
        kernel,
        out_shape=jax.ShapeDtypeStruct((STEPS, WIDE), jnp.float32),
        in_specs=[VMEM, VMEM],
        out_specs=VMEM,
        scratch_shapes=[pltpu.VMEM((STEPS + PAD, WIDE), jnp.float32)],
        compiler_params=pltpu.CompilerParams(vmem_limit_bytes=16 * 1024 * 1024),
        cost_estimate=pl.CostEstimate(
            flops=2 * (STEPS + PAD) * WIDE * WIDE * CHUNKS, bytes_accessed=7 << 20, transcendentals=0
        ),
    )(history, matrix)


def on_device(newest, earlier, lag_matrices):
    swap = [(0, 1), (1, 0)]

    matrix = lag_matrices[0]
    sibling_matrix = lax.ppermute(matrix, "c", swap)

    own = jnp.broadcast_to(message(newest, earlier)[None], (LIKES, MESSAGE, HALF))
    like = lax.all_to_all(own, AXES, 0, 0, tiled=True, axis_index_groups=groups_of(True))
    packed, sibling_columns = pack(like, sibling_matrix)
    history = lax.all_to_all(packed, AXES, 0, 0, tiled=True, axis_index_groups=groups_of(False))

    for_sibling = product(history, sibling_columns)
    from_sibling = lax.ppermute(for_sibling, "c", swap)
    terms = product(history, matrix) + from_sibling
    terms = lax.all_to_all(terms.reshape(16, OWN, WIDE), LAG, 0, 0, tiled=True)
    return jnp.sum(terms, axis=0)


def solution(mesh):
    fine = Mesh(mesh.devices.reshape(SIZES), AXES)
    in_specs = (P(LAG, ROW), P(None, ROW), P(LAG, ROW, None))
    return jax.shard_map(on_device, mesh=fine, in_specs=in_specs, out_specs=P(LAG, ROW), check_vma=False)
```

```python
import functools

import jax
import jax.numpy as jnp
from jax import lax
from jax.experimental import pallas as pl
from jax.experimental.pallas import tpu as pltpu
from jax.sharding import Mesh, PartitionSpec as P

AXES = ("yh", "yl", "h", "zh", "zl", "l", "c")
SIZES = (4, 2, 2, 4, 2, 2, 2)
LAG = ("yh", "yl", "h")
ROW = ("zh", "zl", "l", "c")

RINGS = (4, 8, 8)
STEPS = 512
OWN = 32
PAD = 16
WIDE = 256
HALF = 128
BLOCK = 64
MESSAGE = 72
CHUNKS = 16
LIKES = 32
PACKED = LIKES * BLOCK + 4 * PAD
VMEM = pl.BlockSpec(memory_space=pltpu.VMEM)


def split_ring(u, size):
    return u // 2, (u % 2 + u // (size // 2)) % 2


def join_ring(pair, side, size):
    return 2 * pair + (side + 2 * pair // (size // 2)) % 2


def device_index(pairs, sides, c):
    x, y, z = ((join_ring(p, s, n) - c) % n for p, s, n in zip(pairs, sides, RINGS))
    return (((y * 2 + x // 2) * 8 + z) * 2 + x % 2) * 2 + c


def groups_of(same_side):
    all_pairs = [(px, py, pz) for py in range(4) for px in range(2) for pz in range(4)]
    all_sides = [(ax, ay, az) for ax in range(2) for ay in range(2) for az in range(2)]
    if same_side:
        return [[device_index(p, s, c) for p in all_pairs] for c in range(2) for s in all_sides]
    return [[device_index(p, s, c) for s in all_sides] for c in range(2) for p in all_pairs]


def lag_index():
    return (lax.axis_index("yh") * 2 + lax.axis_index("yl")) * 2 + lax.axis_index("h")


def columns_of(chunk, core):
    start = (2 * chunk + core) * WIDE
    return pl.ds(start if isinstance(core, int) else pl.multiple_of(start, WIDE), WIDE)


def position():
    c = lax.axis_index("c")
    x = lax.axis_index("h") * 2 + lax.axis_index("l")
    y = lax.axis_index("yh") * 2 + lax.axis_index("yl")
    z = lax.axis_index("zh") * 2 + lax.axis_index("zl")
    return [split_ring((v + c) % n, n) for v, n in zip((x, y, z), RINGS)]


def message_kernel(newest, earlier, out):
    (_, ax), (py, ay), _ = position()
    before = earlier[...].astype(jnp.float32)
    row = lax.broadcasted_iota(jnp.int32, before.shape, 0) + 1
    mine = jnp.sum(jnp.where(row == ax * 8 + ay * 4 + py, before, 0.0), axis=0, keepdims=True)
    place = lax.broadcasted_iota(jnp.int32, (MESSAGE - BLOCK, HALF), 0)
    extra = jnp.where(place == 0, mine[:, :HALF], jnp.where(place == 1, mine[:, HALF:], 0.0))
    block = newest[...]
    whole = jnp.concatenate([block[:, :HALF], block[:, HALF:], extra.astype(block.dtype)], axis=0)
    for copy in range(LIKES):
        out[copy] = whole


def message(newest, earlier):
    return pl.pallas_call(
        message_kernel,
        out_shape=jax.ShapeDtypeStruct((LIKES, MESSAGE, HALF), newest.dtype),
        in_specs=[VMEM, VMEM],
        out_specs=VMEM,
    )(newest, earlier)


def column_copies(matrix, held, arrived):
    return [
        pltpu.make_async_copy(
            matrix.at[:, columns_of(chunk, lax.axis_index("c"))], held.at[chunk], arrived.at[chunk]
        )
        for chunk in range(CHUNKS)
    ]


def pack_kernel(like, sibling_matrix, out, columns, arrived):
    copies = column_copies(sibling_matrix, columns, arrived)
    for copy in copies:
        copy.start()
    place = lax.broadcasted_iota(jnp.int32, (PAD, HALF), 0)
    for pz in range(4):
        before = jnp.zeros((PAD, HALF), jnp.float32)
        for py in range(4):
            for px in range(2):
                index = (py * 2 + px) * 4 + pz
                whole = like[index]
                for copy in range(8):
                    out[copy, index * BLOCK : (index + 1) * BLOCK, :] = whole[:BLOCK]
                extra = whole[BLOCK:].astype(jnp.float32)
                for half in range(2):
                    before = jnp.where(place == px * 8 + half * 4 + py, extra[half : half + 1], before)
        start = LIKES * BLOCK + pz * PAD
        for copy in range(8):
            out[copy, start : start + PAD, :] = before.astype(like.dtype)
    for copy in copies:
        copy.wait()


def pack(like, sibling_matrix):
    return pl.pallas_call(
        pack_kernel,
        out_shape=[
            jax.ShapeDtypeStruct((8, PACKED, HALF), like.dtype),
            jax.ShapeDtypeStruct((CHUNKS, WIDE, WIDE), like.dtype),
        ],
        in_specs=[VMEM, pl.BlockSpec(memory_space=pl.ANY)],
        out_specs=[VMEM, VMEM],
        scratch_shapes=[pltpu.SemaphoreType.DMA((CHUNKS,))],
        compiler_params=pltpu.CompilerParams(vmem_limit_bytes=16 * 1024 * 1024),
    )(like, sibling_matrix)


def window_chunk(core, history, chunk):
    z, l = chunk // 2, chunk % 2
    pz, az = split_ring((z + core) % 8, 8)
    sides = {}
    for h in range(2):
        px, ax = split_ring((2 * h + l + core) % 4, 4)
        sides[ax] = px
    start = LIKES * BLOCK + pz * PAD
    before = [
        (sides[ax] * 8, history[ax * 4 + ay * 2 + az, start : start + PAD, :].astype(jnp.float32))
        for ax in range(2)
        for ay in range(2)
    ]
    halves = []
    for half in range(2):
        pieces = [rows[first + half * 4 : first + half * 4 + 4] for first, rows in before]
        blocks = [jnp.concatenate(pieces, axis=0).astype(history.dtype)]
        for y in range(8):
            py, ay = split_ring((y + core) % 8, 8)
            for h in range(2):
                px, ax = split_ring((2 * h + l + core) % 4, 4)
                first = ((py * 2 + px) * 4 + pz) * BLOCK + half * OWN
                blocks.append(history[ax * 4 + ay * 2 + az, first : first + OWN, :])
        halves.append(jnp.concatenate(blocks, axis=0))
    return jnp.concatenate(halves, axis=1)


def product_kernel(matrix_chunk, history, matrix, out, total):
    for core in range(2):

        @pl.when(lax.axis_index("c") == core)
        def _():
            for chunk in range(CHUNKS):
                term = lax.dot_general(
                    window_chunk(core, history, chunk),
                    matrix_chunk(matrix, core, chunk),
                    (((1,), (1,)), ((), ())),
                    preferred_element_type=jnp.float32,
                )
                total[...] = term if chunk == 0 else total[...] + term

    rows = STEPS + PAD
    out[...] = pltpu.roll(total[...], rows - PAD + lag_index(), 0)[:STEPS]


def of_block(matrix, core, chunk):
    return matrix[:, columns_of(chunk, core)]


def of_columns(matrix, core, chunk):
    return matrix[chunk]


def product(matrix_chunk, history, matrix):
    return pl.pallas_call(
        functools.partial(product_kernel, matrix_chunk),
        out_shape=jax.ShapeDtypeStruct((STEPS, WIDE), jnp.float32),
        in_specs=[VMEM, VMEM],
        out_specs=VMEM,
        scratch_shapes=[pltpu.VMEM((STEPS + PAD, WIDE), jnp.float32)],
        compiler_params=pltpu.CompilerParams(vmem_limit_bytes=16 * 1024 * 1024),
        cost_estimate=pl.CostEstimate(
            flops=2 * (STEPS + PAD) * WIDE * WIDE * CHUNKS, bytes_accessed=7 << 20, transcendentals=0
        ),
    )(history, matrix)


def on_device(newest, earlier, lag_matrices):
    swap = [(0, 1), (1, 0)]

    matrix = lag_matrices[0]
    sibling_matrix = lax.ppermute(matrix, "c", swap)

    like = lax.all_to_all(message(newest, earlier), AXES, 0, 0, tiled=True, axis_index_groups=groups_of(True))
    packed, sibling_columns = pack(like, sibling_matrix)
    history = lax.all_to_all(packed, AXES, 0, 0, tiled=True, axis_index_groups=groups_of(False))

    for_sibling = product(of_columns, history, sibling_columns)
    from_sibling = lax.ppermute(for_sibling, "c", swap)
    terms = product(of_block, history, matrix) + from_sibling
    terms = lax.all_to_all(terms.reshape(16, OWN, WIDE), LAG, 0, 0, tiled=True)
    return jnp.sum(terms, axis=0)


def solution(mesh):
    fine = Mesh(mesh.devices.reshape(SIZES), AXES)
    in_specs = (P(LAG, ROW), P(None, ROW), P(LAG, ROW, None))
    return jax.shard_map(on_device, mesh=fine, in_specs=in_specs, out_specs=P(LAG, ROW), check_vma=False)
```

```python
import jax
import jax.numpy as jnp
from jax import lax
from jax.experimental import pallas as pl
from jax.experimental.pallas import tpu as pltpu
from jax.sharding import Mesh, PartitionSpec as P

AXES = ("yh", "yl", "h", "zh", "zl", "l", "c")
SIZES = (4, 2, 2, 4, 2, 2, 2)
LAG = ("yh", "yl", "h")
ROW = ("zh", "zl", "l", "c")

RINGS = (4, 8, 8)
STEPS = 512
OWN = 32
PAD = 16
WIDE = 256
HALF = 128
BLOCK = 64
MESSAGE = 72
CHUNKS = 16
LIKES = 32
PACKED = LIKES * BLOCK + 4 * PAD
VMEM = pl.BlockSpec(memory_space=pltpu.VMEM)


def split_ring(u, size):
    return u // 2, (u % 2 + u // (size // 2)) % 2


def join_ring(pair, side, size):
    return 2 * pair + (side + 2 * pair // (size // 2)) % 2


def device_index(pairs, sides, c):
    x, y, z = ((join_ring(p, s, n) - c) % n for p, s, n in zip(pairs, sides, RINGS))
    return (((y * 2 + x // 2) * 8 + z) * 2 + x % 2) * 2 + c


def groups_of(same_side):
    all_pairs = [(px, py, pz) for py in range(4) for px in range(2) for pz in range(4)]
    all_sides = [(ax, ay, az) for ax in range(2) for ay in range(2) for az in range(2)]
    if same_side:
        return [[device_index(p, s, c) for p in all_pairs] for c in range(2) for s in all_sides]
    return [[device_index(p, s, c) for s in all_sides] for c in range(2) for p in all_pairs]


def lag_index():
    return (lax.axis_index("yh") * 2 + lax.axis_index("yl")) * 2 + lax.axis_index("h")


def columns_of(chunk, core):
    start = (2 * chunk + core) * WIDE
    return slice(start, start + WIDE)


def position():
    c = lax.axis_index("c")
    x = lax.axis_index("h") * 2 + lax.axis_index("l")
    y = lax.axis_index("yh") * 2 + lax.axis_index("yl")
    z = lax.axis_index("zh") * 2 + lax.axis_index("zl")
    return [split_ring((v + c) % n, n) for v, n in zip((x, y, z), RINGS)]


def message_kernel(newest, earlier, out):
    (_, ax), (py, ay), _ = position()
    before = earlier[...].astype(jnp.float32)
    row = lax.broadcasted_iota(jnp.int32, before.shape, 0) + 1
    mine = jnp.sum(jnp.where(row == ax * 8 + ay * 4 + py, before, 0.0), axis=0, keepdims=True)
    place = lax.broadcasted_iota(jnp.int32, (MESSAGE - BLOCK, HALF), 0)
    extra = jnp.where(place == 0, mine[:, :HALF], jnp.where(place == 1, mine[:, HALF:], 0.0))
    block = newest[...]
    whole = jnp.concatenate([block[:, :HALF], block[:, HALF:], extra.astype(block.dtype)], axis=0)
    for copy in range(LIKES):
        out[copy] = whole


def message(newest, earlier):
    return pl.pallas_call(
        message_kernel,
        out_shape=jax.ShapeDtypeStruct((LIKES, MESSAGE, HALF), newest.dtype),
        in_specs=[VMEM, VMEM],
        out_specs=VMEM,
        compiler_params=pltpu.CompilerParams(vmem_limit_bytes=4 * 1024 * 1024),
    )(newest, earlier)


def pack_kernel(like, sibling_matrix, out):
    place = lax.broadcasted_iota(jnp.int32, (PAD, HALF), 0)
    for pz in range(4):
        before = jnp.zeros((PAD, HALF), jnp.float32)
        for py in range(4):
            for px in range(2):
                index = (py * 2 + px) * 4 + pz
                whole = like[index]
                for copy in range(8):
                    out[copy, index * BLOCK : (index + 1) * BLOCK, :] = whole[:BLOCK]
                extra = whole[BLOCK:].astype(jnp.float32)
                for half in range(2):
                    before = jnp.where(place == px * 8 + half * 4 + py, extra[half : half + 1], before)
        start = LIKES * BLOCK + pz * PAD
        for copy in range(8):
            out[copy, start : start + PAD, :] = before.astype(like.dtype)


def pack(like, sibling_matrix):
    return pl.pallas_call(
        pack_kernel,
        out_shape=jax.ShapeDtypeStruct((8, PACKED, HALF), like.dtype),
        in_specs=[VMEM, pl.BlockSpec(memory_space=pl.ANY)],
        out_specs=VMEM,
        compiler_params=pltpu.CompilerParams(vmem_limit_bytes=12 * 1024 * 1024),
    )(like, sibling_matrix)


def window_chunk(core, history, chunk):
    z, l = chunk // 2, chunk % 2
    pz, az = split_ring((z + core) % 8, 8)
    sides = {}
    for h in range(2):
        px, ax = split_ring((2 * h + l + core) % 4, 4)
        sides[ax] = px
    start = LIKES * BLOCK + pz * PAD
    before = [
        (sides[ax] * 8, history[ax * 4 + ay * 2 + az, start : start + PAD, :].astype(jnp.float32))
        for ax in range(2)
        for ay in range(2)
    ]
    halves = []
    for half in range(2):
        pieces = [rows[first + half * 4 : first + half * 4 + 4] for first, rows in before]
        blocks = [jnp.concatenate(pieces, axis=0).astype(history.dtype)]
        for y in range(8):
            py, ay = split_ring((y + core) % 8, 8)
            for h in range(2):
                px, ax = split_ring((2 * h + l + core) % 4, 4)
                first = ((py * 2 + px) * 4 + pz) * BLOCK + half * OWN
                blocks.append(history[ax * 4 + ay * 2 + az, first : first + OWN, :])
        halves.append(jnp.concatenate(blocks, axis=0))
    return jnp.concatenate(halves, axis=1)


def product_kernel(history, matrix, out, total):
    for core in range(2):

        @pl.when(lax.axis_index("c") == core)
        def _():
            for chunk in range(CHUNKS):
                term = lax.dot_general(
                    window_chunk(core, history, chunk),
                    matrix[:, columns_of(chunk, core)],
                    (((1,), (1,)), ((), ())),
                    preferred_element_type=jnp.float32,
                )
                total[...] = term if chunk == 0 else total[...] + term

    rows = STEPS + PAD
    out[...] = pltpu.roll(total[...], rows - PAD + lag_index(), 0)[:STEPS]


def product(history, matrix):
    return pl.pallas_call(
        product_kernel,
        out_shape=jax.ShapeDtypeStruct((STEPS, WIDE), jnp.float32),
        in_specs=[VMEM, VMEM],
        out_specs=VMEM,
        scratch_shapes=[pltpu.VMEM((STEPS + PAD, WIDE), jnp.float32)],
        compiler_params=pltpu.CompilerParams(vmem_limit_bytes=12 * 1024 * 1024),
        cost_estimate=pl.CostEstimate(
            flops=2 * (STEPS + PAD) * WIDE * WIDE * CHUNKS, bytes_accessed=7 << 20, transcendentals=0
        ),
    )(history, matrix)


def on_device(newest, earlier, lag_matrices):
    swap = [(0, 1), (1, 0)]

    matrix = lag_matrices[0]
    sibling_matrix = lax.ppermute(matrix, "c", swap)

    like = lax.all_to_all(message(newest, earlier), AXES, 0, 0, tiled=True, axis_index_groups=groups_of(True))
    packed = pack(like, sibling_matrix)
    history = lax.all_to_all(packed, AXES, 0, 0, tiled=True, axis_index_groups=groups_of(False))

    for_sibling = product(history, sibling_matrix)
    from_sibling = lax.ppermute(for_sibling, "c", swap)
    terms = product(history, matrix) + from_sibling
    terms = lax.all_to_all(terms.reshape(16, OWN, WIDE), LAG, 0, 0, tiled=True)
    return jnp.sum(terms, axis=0)


def solution(mesh):
    fine = Mesh(mesh.devices.reshape(SIZES), AXES)
    in_specs = (P(LAG, ROW), P(None, ROW), P(LAG, ROW, None))
    return jax.shard_map(on_device, mesh=fine, in_specs=in_specs, out_specs=P(LAG, ROW), check_vma=False)
```

```python
import jax
import jax.numpy as jnp
from jax import lax
from jax.experimental import pallas as pl
from jax.experimental.pallas import tpu as pltpu
from jax.sharding import Mesh, PartitionSpec as P

AXES = ("yh", "yl", "h", "zh", "zl", "l", "c")
SIZES = (4, 2, 2, 4, 2, 2, 2)
LAG = ("yh", "yl", "h")
ROW = ("zh", "zl", "l", "c")

RINGS = (4, 8, 8)
STEPS = 512
OWN = 32
PAD = 16
WIDE = 256
HALF = 128
BLOCK = 64
MESSAGE = 72
CHUNKS = 16
LIKES = 32
PACKED = LIKES * BLOCK + 4 * PAD
VMEM = pl.BlockSpec(memory_space=pltpu.VMEM)


def split_ring(u, size):
    return u // 2, (u % 2 + u // (size // 2)) % 2


def join_ring(pair, side, size):
    return 2 * pair + (side + 2 * pair // (size // 2)) % 2


def device_index(pairs, sides, c):
    x, y, z = ((join_ring(p, s, n) - c) % n for p, s, n in zip(pairs, sides, RINGS))
    return (((y * 2 + x // 2) * 8 + z) * 2 + x % 2) * 2 + c


def groups_of(same_side):
    all_pairs = [(px, py, pz) for py in range(4) for px in range(2) for pz in range(4)]
    all_sides = [(ax, ay, az) for ax in range(2) for ay in range(2) for az in range(2)]
    if same_side:
        return [[device_index(p, s, c) for p in all_pairs] for c in range(2) for s in all_sides]
    return [[device_index(p, s, c) for s in all_sides] for c in range(2) for p in all_pairs]


def lag_index():
    return (lax.axis_index("yh") * 2 + lax.axis_index("yl")) * 2 + lax.axis_index("h")


def columns_of(chunk, core):
    start = (2 * chunk + core) * WIDE
    return slice(start, start + WIDE)


def position():
    c = lax.axis_index("c")
    x = lax.axis_index("h") * 2 + lax.axis_index("l")
    y = lax.axis_index("yh") * 2 + lax.axis_index("yl")
    z = lax.axis_index("zh") * 2 + lax.axis_index("zl")
    return [split_ring((v + c) % n, n) for v, n in zip((x, y, z), RINGS)]


def message_kernel(newest, earlier, out):
    (_, ax), (py, ay), _ = position()
    before = earlier[...].astype(jnp.float32)
    row = lax.broadcasted_iota(jnp.int32, before.shape, 0) + 1
    mine = jnp.sum(jnp.where(row == ax * 8 + ay * 4 + py, before, 0.0), axis=0, keepdims=True)
    place = lax.broadcasted_iota(jnp.int32, (MESSAGE - BLOCK, HALF), 0)
    extra = jnp.where(place == 0, mine[:, :HALF], jnp.where(place == 1, mine[:, HALF:], 0.0))
    block = newest[...]
    whole = jnp.concatenate([block[:, :HALF], block[:, HALF:], extra.astype(block.dtype)], axis=0)
    for copy in range(LIKES):
        out[copy] = whole


def message(newest, earlier):
    return pl.pallas_call(
        message_kernel,
        out_shape=jax.ShapeDtypeStruct((LIKES, MESSAGE, HALF), newest.dtype),
        in_specs=[VMEM, VMEM],
        out_specs=VMEM,
        compiler_params=pltpu.CompilerParams(vmem_limit_bytes=4 * 1024 * 1024),
    )(newest, earlier)


def pack_kernel(like, sibling_matrix, out):
    place = lax.broadcasted_iota(jnp.int32, (PAD, HALF), 0)
    for pz in range(4):
        before = jnp.zeros((PAD, HALF), jnp.float32)
        for py in range(4):
            for px in range(2):
                index = (py * 2 + px) * 4 + pz
                whole = like[index]
                for copy in range(8):
                    out[copy, index * BLOCK : (index + 1) * BLOCK, :] = whole[:BLOCK]
                extra = whole[BLOCK:].astype(jnp.float32)
                for half in range(2):
                    before = jnp.where(place == px * 8 + half * 4 + py, extra[half : half + 1], before)
        start = LIKES * BLOCK + pz * PAD
        for copy in range(8):
            out[copy, start : start + PAD, :] = before.astype(like.dtype)


def pack(like, sibling_matrix):
    return pl.pallas_call(
        pack_kernel,
        out_shape=jax.ShapeDtypeStruct((8, PACKED, HALF), like.dtype),
        in_specs=[VMEM, pl.BlockSpec(memory_space=pl.ANY)],
        out_specs=VMEM,
        compiler_params=pltpu.CompilerParams(vmem_limit_bytes=12 * 1024 * 1024),
    )(like, sibling_matrix)


def window_chunk(core, history, chunk):
    z, l = chunk // 2, chunk % 2
    pz, az = split_ring((z + core) % 8, 8)
    sides = {}
    for h in range(2):
        px, ax = split_ring((2 * h + l + core) % 4, 4)
        sides[ax] = px
    start = LIKES * BLOCK + pz * PAD
    before = [
        (sides[ax] * 8, history[ax * 4 + ay * 2 + az, start : start + PAD, :].astype(jnp.float32))
        for ax in range(2)
        for ay in range(2)
    ]
    halves = []
    for half in range(2):
        pieces = [rows[first + half * 4 : first + half * 4 + 4] for first, rows in before]
        blocks = [jnp.concatenate(pieces, axis=0).astype(history.dtype)]
        for y in range(8):
            py, ay = split_ring((y + core) % 8, 8)
            for h in range(2):
                px, ax = split_ring((2 * h + l + core) % 4, 4)
                first = ((py * 2 + px) * 4 + pz) * BLOCK + half * OWN
                blocks.append(history[ax * 4 + ay * 2 + az, first : first + OWN, :])
        halves.append(jnp.concatenate(blocks, axis=0))
    return jnp.concatenate(halves, axis=1)


def product_kernel(history, matrix, out, total):
    for core in range(2):

        @pl.when(lax.axis_index("c") == core)
        def _():
            for chunk in range(0, CHUNKS, 2):
                both = (chunk, chunk + 1)
                term = lax.dot_general(
                    jnp.concatenate([window_chunk(core, history, k) for k in both], axis=1),
                    jnp.concatenate([matrix[:, columns_of(k, core)] for k in both], axis=1),
                    (((1,), (1,)), ((), ())),
                    preferred_element_type=jnp.float32,
                )
                total[...] = term if chunk == 0 else total[...] + term

    rows = STEPS + PAD
    out[...] = pltpu.roll(total[...], rows - PAD + lag_index(), 0)[:STEPS]


def product(history, matrix):
    return pl.pallas_call(
        product_kernel,
        out_shape=jax.ShapeDtypeStruct((STEPS, WIDE), jnp.float32),
        in_specs=[VMEM, VMEM],
        out_specs=VMEM,
        scratch_shapes=[pltpu.VMEM((STEPS + PAD, WIDE), jnp.float32)],
        compiler_params=pltpu.CompilerParams(vmem_limit_bytes=12 * 1024 * 1024),
        cost_estimate=pl.CostEstimate(
            flops=2 * (STEPS + PAD) * WIDE * WIDE * CHUNKS, bytes_accessed=7 << 20, transcendentals=0
        ),
    )(history, matrix)


def on_device(newest, earlier, lag_matrices):
    swap = [(0, 1), (1, 0)]

    own, matrix = lax.optimization_barrier((message(newest, earlier), lag_matrices[0]))
    sibling_matrix = lax.ppermute(matrix, "c", swap)

    like = lax.all_to_all(own, AXES, 0, 0, tiled=True, axis_index_groups=groups_of(True))
    packed = pack(like, sibling_matrix)
    history = lax.all_to_all(packed, AXES, 0, 0, tiled=True, axis_index_groups=groups_of(False))

    for_sibling = product(history, sibling_matrix)
    from_sibling = lax.ppermute(for_sibling, "c", swap)
    terms = product(history, matrix) + from_sibling
    terms = lax.all_to_all(terms.reshape(16, OWN, WIDE), LAG, 0, 0, tiled=True)
    return jnp.sum(terms, axis=0)


def solution(mesh):
    fine = Mesh(mesh.devices.reshape(SIZES), AXES)
    in_specs = (P(LAG, ROW), P(None, ROW), P(LAG, ROW, None))
    return jax.shard_map(on_device, mesh=fine, in_specs=in_specs, out_specs=P(LAG, ROW), check_vma=False)
```
